32 devices in a mesh: grp: 4 (over y, core), row: 8 (over z, x).
Axes of the slice: x: 2, y: 2, z: 4, core: 2. Of those that a mesh axis runs over, the one named last changes fastest.
Arguments:
- a_blocks: bfloat16 [81920, 512], P(('grp', 'row')), may hold values from -0.25 to 0.25
- a_cols: int32 [1280, 8], P(('grp', 'row')), may hold values from 0 to 1279, as said below
- a_count: int32 [1280], P(('grp', 'row')), may hold values from 2 to 8, as said below
- p_blocks: bfloat16 [81920, 256], P(('grp', 'row')), may hold values from -0.75 to 0.75
- p_cols: int32 [1280, 4], P(('grp', 'row')), may hold values from 0 to 319, as said below
- q2_blocks: bfloat16 [320, 4096], P(('grp', 'row')), may hold values from -0.75 to 0.75
- agg3: int32 [320], P(('grp', 'row')), may hold values from 0 to 47, as said below
Outputs:
- level2_op: bfloat16 [20480, 3200], P(('grp', 'row'))
- level3_op: float32 [3072, 2304], P('grp')
The draws below stay inside these ranges and needn't reach their ends.
Inputs may be any that keep to these rules, and one draw needn't show every extreme that they name: a_cols[i, 0] = i, and every a_cols[i, k] differs from i by at most 40. `a_count`: block rows i with i % 40 == 0 use all 8 blocks. `p_cols`: the 4 entries of a row are distinct and lie from 10 (i // 40) to 10 (i // 40 + 2) - 1 for block row i. agg3[c] lies from 12 g to 12 (g + 1) - 1 with g = c // 80.
All inputs are finite; a program needn't handle non-finite values.
Results may differ from the reference program's by a relative error of at most 0.0058.
Values may be sent and summed in bfloat16 or wider, within the bound.
A program may use at most 128 MiB of HBM per device.

```python
import jax
import jax.numpy as jnp
from jax import lax

B = 64
KA = 8
KP = 4
A3G = 12
BR = 40
CR = 10
N1 = 1280
N2 = 320
N3 = 48
N_GRP = 4
N_ROW = 8


def draw_a_cols(key, part):
    key = jax.random.fold_in(key, 11)
    rows_all = jnp.arange(N1, dtype=jnp.int32)
    offsets = jax.random.randint(key, (N1, KA), -BR, BR + 1, dtype=jnp.int32)
    columns = jnp.clip(rows_all[:, None] + offsets, 0, N1 - 1)
    first = (jnp.arange(KA, dtype=jnp.int32) == 0)[None, :]
    return jnp.where(first, rows_all[:, None], columns).astype(jnp.int32)


def draw_a_count(key, part):
    key = jax.random.fold_in(key, 17)
    counts = jax.random.randint(key, (N1,), 2, KA + 1, dtype=jnp.int32)
    rows_all = jnp.arange(N1, dtype=jnp.int32)
    return jnp.where(rows_all % BR == 0, KA, counts).astype(jnp.int32)


def draw_p_cols(key, part):
    key = jax.random.fold_in(key, 23)
    keys = jax.random.split(key, N1)
    wide_pick = jax.vmap(lambda k: jax.random.permutation(k, 2 * CR)[:KP])(keys)
    near_pick = jax.vmap(lambda k: jax.random.permutation(jax.random.fold_in(k, 1), CR)[:KP])(keys)
    device = jnp.arange(N1, dtype=jnp.int32) // BR
    last = device == N1 // BR - 1
    pick = jnp.where(last[:, None], near_pick, wide_pick)
    return (device[:, None] * CR + pick).astype(jnp.int32)


def draw_agg3(key, part):
    key = jax.random.fold_in(key, 29)
    group_of = jnp.arange(N2, dtype=jnp.int32) // (CR * N_ROW)
    inside = jax.random.randint(key, (N2,), 0, A3G, dtype=jnp.int32)
    return (group_of * A3G + inside).astype(jnp.int32)


def steps_of(rng, extent, cuts, smallest, largest):
    loudness = 1.0
    for position, blocks in cuts:
        draws = jax.random.uniform(jax.random.fold_in(jax.random.fold_in(rng, 6), position), (blocks,), jnp.float32, smallest / len(cuts), largest / len(cuts))
        loudness = loudness * jnp.repeat(jnp.exp(draws), extent[position] // blocks).reshape((-1,) + (1,) * (len(extent) - 1 - position))
    return loudness


def noise(own_key, dims, spread, reach, shards=(), held_as=jnp.bfloat16):
    level = steps_of(own_key, dims, shards, -0.22, 0.18) if shards else 1.0
    array = jax.random.normal(own_key, dims, jnp.float32) * spread * level
    return jnp.minimum(jnp.maximum(array, -reach), reach).astype(held_as)


def setup_inputs(seed: int = 0) -> dict:
    key_of = jax.random.split(jax.random.key(seed), 8)
    a_blocks = noise(key_of[0], (N1 * B, KA * B), (KA * B) ** -0.5, 0.25, ((0, 32),))
    a_cols = draw_a_cols(jax.random.fold_in(key_of[7], 71), 0)
    a_count = draw_a_count(jax.random.fold_in(key_of[7], 71), 0)
    p_blocks = noise(key_of[3], (N1 * B, KP * B), B ** -0.5, 0.75, ((0, 32),))
    p_cols = draw_p_cols(jax.random.fold_in(key_of[7], 71), 0)
    q2_blocks = noise(key_of[5], (N2, B * B), B ** -0.5, 0.75, ((0, 32),))
    agg3 = draw_agg3(jax.random.fold_in(key_of[7], 71), 0)
    return {"a_blocks": a_blocks, "a_cols": a_cols, "a_count": a_count, "p_blocks": p_blocks, "p_cols": p_cols, "q2_blocks": q2_blocks, "agg3": agg3}


def reference(a_blocks, a_cols, a_count, p_blocks, p_cols, q2_blocks, agg3):
    devices_all = N_GRP * N_ROW
    highest_precision_flag = lax.Precision.HIGHEST
    third_level_operator = a_blocks.reshape(N1, B, KA * B)
    p_three = p_blocks.reshape(N1, B, KP * B)
    wide_ids = jnp.arange(4 * CR, dtype=jnp.int32)
    own_ids = jnp.arange(2 * CR, dtype=jnp.int32)
    slots = jnp.arange(KA, dtype=jnp.int32)
    band = CR * B

    def fine_device(pending, device):
        start = (device * BR).astype(jnp.int32)
        amat = lax.dynamic_slice_in_dim(third_level_operator, start, BR, 0).reshape(BR, B, KA, B).astype(jnp.float32)
        cols = lax.dynamic_slice_in_dim(a_cols, start, BR, 0)
        count = lax.dynamic_slice_in_dim(a_count, start, BR, 0)
        keep = slots[None, :] < count[:, None]
        amat = jnp.where(keep[:, None, :, None], amat, jnp.zeros_like(amat))
        prow = p_three[cols].astype(jnp.float32)
        pattern = p_cols[cols] - (device - 1) * CR
        hot = (pattern[..., None] == wide_ids).astype(jnp.float32)
        prod = jnp.einsum("rfkg,rkgq->rkfq", amat, prow, precision=highest_precision_flag).reshape(BR, KA, B, KP, B)
        wide = jnp.einsum("rkfmq,rkmc->rfcq", prod, hot, precision=highest_precision_flag).astype(jnp.bfloat16)
        wide = wide.reshape(BR, B, 4 * CR * B).astype(jnp.float32)
        pmat = lax.dynamic_slice_in_dim(p_three, start, BR, 0).reshape(BR, B, KP, B).astype(jnp.float32)
        part = jnp.einsum("rfmq,rfx->rmqx", pmat, wide, precision=highest_precision_flag)
        pcols = lax.dynamic_slice_in_dim(p_cols, start, BR, 0)
        owner_hot = ((pcols - device * CR)[..., None] == own_ids).astype(jnp.float32)
        total = jnp.einsum("rmt,rmqx->tqx", owner_hot, part, precision=highest_precision_flag).reshape(2 * band, 4 * band)
        level2 = jnp.pad(total[:band], ((0, 0), (band, 0))) + jnp.pad(pending, ((0, 0), (0, band)))
        return total[band:], level2.astype(jnp.bfloat16)

    start_pending = jnp.zeros((band, 4 * band), jnp.float32)
    unused, pieces = lax.scan(fine_device, start_pending, jnp.arange(devices_all, dtype=jnp.int32))
    level2_op = pieces.reshape(N2 * B, 5 * band)

    blocks_q = q2_blocks.reshape(N2, B, B)
    group_of = jnp.arange(N2, dtype=jnp.int32) // (CR * N_ROW)
    picks = (agg3 - group_of * A3G)[:, None] == jnp.arange(A3G, dtype=jnp.int32)
    dense_q = jnp.where(picks[:, None, :, None], blocks_q[:, :, None, :], jnp.zeros((), jnp.bfloat16))
    dense_q = dense_q.reshape(N2 * B, A3G * B)
    padded_q = jnp.pad(dense_q, ((2 * band, 2 * band), (0, 0)))

    def coarse_device(total, device):
        group = device // N_ROW
        ext_q = lax.dynamic_slice_in_dim(padded_q, (device * band).astype(jnp.int32), 5 * band, 0)
        rows_list = []
        for source_partition in range(5):
            piece = ext_q[source_partition * band:(source_partition + 1) * band]
            shift_group = (device + source_partition - 2) // N_ROW - group + 1
            blank = jnp.zeros_like(piece)
            rows_list.append(jnp.concatenate([jnp.where(shift_group == slot, piece, blank) for slot in range(3)], axis=1))
        window = jnp.concatenate(rows_list, axis=0)
        mine = lax.dynamic_slice_in_dim(level2_op, (device * band).astype(jnp.int32), band, 0)
        mixed_precision_result = jnp.dot(mine, window, preferred_element_type=jnp.float32).astype(jnp.bfloat16)
        own_q = lax.dynamic_slice_in_dim(dense_q, (device * band).astype(jnp.int32), band, 0)
        share_sum = jnp.dot(own_q.T, mixed_precision_result, preferred_element_type=jnp.float32)
        offset = (group * A3G * B).astype(jnp.int32)
        current = lax.dynamic_slice_in_dim(total, offset, A3G * B, 0)
        return lax.dynamic_update_slice_in_dim(total, current + share_sum, offset, 0), None

    start_total = jnp.zeros((N3 * B, 3 * A3G * B), jnp.float32)
    level3_op, unused_out = lax.scan(coarse_device, start_total, jnp.arange(devices_all, dtype=jnp.int32))
    return level2_op, level3_op
```

```python
import functools

import jax
import jax.numpy as jnp
from jax import lax
from jax.experimental import pallas as pl
from jax.experimental.pallas import tpu as pltpu
from jax.sharding import PartitionSpec as P

B = 64
KA = 8
KP = 4
A3G = 12
TR = 4
ALL = ("grp", "row")


def passed_along(array, by):
    devices = lax.axis_size(ALL)
    pairs = [(i, i + by) for i in range(devices) if 0 <= i + by < devices]
    return lax.ppermute(array, ALL, pairs)


def w_kernel(loc_ref, col_ref, a_ref, p_ref, out_ref, *accs):
    step = pl.program_id(0)
    lane = lax.broadcasted_iota(jnp.int32, (B, 2 * B), 1)
    low = lane < B
    half = jnp.where(low, 0, 1)
    for r in range(TR):
        accs[r][...] = jnp.zeros_like(accs[r])
    for k in range(KA):
        for r in range(TR):
            acc = accs[r]
            j = loc_ref[(step * TR + r) * KA + k]
            block = p_ref[pl.ds(pl.multiple_of(j * B, B), B), :]
            prod = jnp.dot(
                a_ref[r * B : (r + 1) * B, k * B : (k + 1) * B],
                block,
                preferred_element_type=jnp.float32,
            )
            for c in range(KP // 2):
                x = prod[:, 2 * c * B : 2 * (c + 1) * B]
                turned = pltpu.roll(x, B, 1)
                pair = (jnp.where(low, x, turned), jnp.where(low, turned, x))
                for e in range(2):
                    t = col_ref[j * KP + 2 * c + e]
                    u = lax.shift_right_logical(t, 1)
                    h = lax.bitwise_and(t, 1)
                    acc[u] = acc[u] + jnp.where(half == h, pair[e], 0.0)
    for r in range(TR):
        for u in range(accs[r].shape[0]):
            out_ref[r * B : (r + 1) * B, 2 * u * B : 2 * (u + 1) * B] = accs[r][u].astype(
                jnp.bfloat16
            )


def w_rows(a, local, cols, ext_p, width):
    rows = a.shape[0]
    steps = rows // (TR * B)
    return pl.pallas_call(
        w_kernel,
        out_shape=jax.ShapeDtypeStruct((rows, width), jnp.bfloat16),
        grid_spec=pltpu.PrefetchScalarGridSpec(
            num_scalar_prefetch=2,
            grid=(steps,),
            in_specs=[
                pl.BlockSpec((TR * B, KA * B), lambda i, *_: (i, 0)),
                pl.BlockSpec(ext_p.shape, lambda i, *_: (0, 0)),
            ],
            out_specs=pl.BlockSpec((TR * B, width), lambda i, *_: (i, 0)),
            scratch_shapes=[pltpu.VMEM((width // (2 * B), B, 2 * B), jnp.float32)] * TR,
        ),
        compiler_params=pltpu.CompilerParams(vmem_limit_bytes=40 * 1024 * 1024),
        cost_estimate=pl.CostEstimate(
            flops=2 * rows * KA * B * KP * B,
            bytes_accessed=2 * (a.size + ext_p.size + rows * width),
            transcendentals=0,
        ),
    )(local, cols, a, ext_p)


def per_device(a_blocks, a_cols, a_count, p_blocks, p_cols, q2_blocks, agg3):
    rows_dev = a_cols.shape[0]
    coarse_dev = q2_blocks.shape[0]
    band = coarse_dev * B
    device = lax.axis_index(ALL)
    row_size = lax.axis_size("row")
    group = device // row_size
    f32, bf16 = jnp.float32, jnp.bfloat16

    near_cols = (p_cols - device * coarse_dev).reshape(-1)
    near_agg = agg3 - group * A3G
    ints = jnp.concatenate([near_agg, near_cols])
    ints = jnp.pad(ints, (0, B * B - ints.shape[0])).astype(bf16)[None, :]
    bundle = jnp.concatenate([q2_blocks, ints], axis=0)
    bundles = [passed_along(bundle, by) for by in (2, 1)]
    bundles += [bundle] + [passed_along(bundle, by) for by in (-1, -2)]
    p_before = passed_along(p_blocks, 1)
    p_after = passed_along(p_blocks, -1)
    ext_ints = jnp.stack([part[coarse_dev, : coarse_dev + rows_dev * KP] for part in bundles])
    ext_ints = ext_ints.astype(jnp.int32)
    steps = jnp.arange(5, dtype=jnp.int32)[:, None]
    ext_agg = ext_ints[:, :coarse_dev] + (device + steps - 2) // row_size * A3G
    ext_agg = ext_agg.reshape(-1)
    ext_cols = ext_ints[1:4, coarse_dev:] + steps[:3] * coarse_dev
    ext_cols = ext_cols.reshape(-1)

    keep = jnp.arange(KA * B, dtype=jnp.int32)[None, :] < (a_count * B)[:, None]
    amat = jnp.where(keep[:, None, :], a_blocks.reshape(rows_dev, B, KA * B), 0).astype(bf16)
    amat = amat.reshape(rows_dev * B, KA * B)
    local = (a_cols - (device - 1) * rows_dev).reshape(-1)
    p_turned = p_blocks.T.reshape(KP, 1, B, rows_dev * B)
    own_t = jnp.repeat((p_cols - device * coarse_dev).T, B, axis=1)
    t_ids = jnp.arange(2 * coarse_dev, dtype=jnp.int32)[:, None, None]
    p_dense = jnp.zeros((2 * coarse_dev, B, rows_dev * B), bf16)
    for m in range(KP):
        p_dense = jnp.where(own_t[m][None, None, :] == t_ids, p_turned[m], p_dense)
    p_dense = p_dense.reshape(2 * band, rows_dev * B)

    ext_q = jnp.concatenate([part[:coarse_dev] for part in bundles], axis=0)
    ext_q = ext_q.reshape(5 * band, B)
    slot = jnp.arange(2 * A3G * B, dtype=jnp.int32) // B
    lanes = (jnp.arange(2 * A3G * B, dtype=jnp.int32) % B)[None, :]
    spread = (jnp.arange(B, dtype=jnp.int32)[:, None] == lanes).astype(bf16)
    wide_q = jnp.dot(ext_q, spread, preferred_element_type=f32).astype(bf16)
    at = ext_agg - group * A3G
    outside = (at < 0) | (at >= A3G)
    at = jnp.where(outside, A3G + jnp.where(at < 0, at + A3G, at - A3G), at)
    at = jnp.repeat(at, B)
    window = jnp.where(at[:, None] == slot[None, :], wide_q, 0).astype(bf16)
    local, amat, p_dense, window = lax.optimization_barrier((local, amat, p_dense, window))
    ext_p = jnp.concatenate([p_before, p_blocks, p_after], axis=0)
    w = w_rows(amat, local, ext_cols, ext_p, 4 * band)
    part = jnp.dot(p_dense[band:], w, preferred_element_type=f32).astype(bf16)
    sent = passed_along(part, 1)
    own = jnp.dot(p_dense[:band], w, preferred_element_type=f32)
    own = lax.optimization_barrier(own)
    level2 = jnp.pad(own, ((0, 0), (band, 0))) + jnp.pad(sent.astype(f32), ((0, 0), (0, band)))
    coarse = level2.astype(bf16)

    v = jnp.dot(coarse, window, preferred_element_type=f32).astype(bf16)
    own_q = window[2 * band : 3 * band, : A3G * B]
    share = lax.dot_general(own_q, v, (((0,), (0,)), ((), ())), preferred_element_type=f32)

    pieces = share.astype(bf16).reshape(row_size, A3G * B // row_size, 2 * A3G * B)
    pieces = lax.all_to_all(pieces, "row", 0, 0).astype(f32)
    middle = jnp.sum(pieces[:, :, : A3G * B], axis=0)
    before = pieces[0, :, A3G * B :] + pieces[1, :, A3G * B :]
    after = pieces[-2, :, A3G * B :] + pieces[-1, :, A3G * B :]
    summed = jnp.concatenate([before, middle, after], axis=1).astype(bf16)
    level3 = lax.all_gather(summed, "row", axis=0, tiled=True).astype(f32)
    return (coarse, level3)


def solution(mesh):
    in_specs = (
        P(ALL, None),
        P(ALL, None),
        P(ALL),
        P(ALL, None),
        P(ALL, None),
        P(ALL, None),
        P(ALL),
    )
    out_specs = (P(ALL, None), P("grp", None))
    return jax.shard_map(
        per_device, mesh=mesh, in_specs=in_specs, out_specs=out_specs, check_vma=False
    )
```

```python
import functools

import jax
import jax.numpy as jnp
from jax import lax
from jax.experimental import pallas as pl
from jax.experimental.pallas import tpu as pltpu
from jax.sharding import PartitionSpec as P

B = 64
KA = 8
KP = 4
A3G = 12
TR = 4
ALL = ("grp", "row")


def passed_along(array, by):
    devices = lax.axis_size(ALL)
    pairs = [(i, i + by) for i in range(devices) if 0 <= i + by < devices]
    return lax.ppermute(array, ALL, pairs)


def w_kernel(loc_ref, col_ref, a_ref, p_ref, out_ref, *accs):
    step = pl.program_id(0)
    lane = lax.broadcasted_iota(jnp.int32, (B, 2 * B), 1)
    low = lane < B
    half = jnp.where(low, 0, 1)
    for r in range(TR):
        accs[r][...] = jnp.zeros_like(accs[r])
    for k in range(KA):
        for r in range(TR):
            acc = accs[r]
            j = loc_ref[(step * TR + r) * KA + k]
            block = p_ref[pl.ds(pl.multiple_of(j * B, B), B), :]
            prod = jnp.dot(
                a_ref[r * B : (r + 1) * B, k * B : (k + 1) * B],
                block,
                preferred_element_type=jnp.float32,
            )
            for c in range(KP // 2):
                x = prod[:, 2 * c * B : 2 * (c + 1) * B]
                turned = pltpu.roll(x, B, 1)
                pair = (jnp.where(low, x, turned), jnp.where(low, turned, x))
                for e in range(2):
                    t = col_ref[j * KP + 2 * c + e]
                    u = lax.shift_right_logical(t, 1)
                    h = lax.bitwise_and(t, 1)
                    acc[u] = acc[u] + jnp.where(half == h, pair[e], 0.0)
    for r in range(TR):
        for u in range(accs[r].shape[0]):
            out_ref[r * B : (r + 1) * B, 2 * u * B : 2 * (u + 1) * B] = accs[r][u].astype(
                jnp.bfloat16
            )


def w_rows(a, local, cols, ext_p, width):
    rows = a.shape[0]
    steps = rows // (TR * B)
    return pl.pallas_call(
        w_kernel,
        out_shape=jax.ShapeDtypeStruct((rows, width), jnp.bfloat16),
        grid_spec=pltpu.PrefetchScalarGridSpec(
            num_scalar_prefetch=2,
            grid=(steps,),
            in_specs=[
                pl.BlockSpec((TR * B, KA * B), lambda i, *_: (i, 0)),
                pl.BlockSpec(ext_p.shape, lambda i, *_: (0, 0)),
            ],
            out_specs=pl.BlockSpec((TR * B, width), lambda i, *_: (i, 0)),
            scratch_shapes=[pltpu.VMEM((width // (2 * B), B, 2 * B), jnp.float32)] * TR,
        ),
        compiler_params=pltpu.CompilerParams(vmem_limit_bytes=40 * 1024 * 1024),
        cost_estimate=pl.CostEstimate(
            flops=2 * rows * KA * B * KP * B,
            bytes_accessed=2 * (a.size + ext_p.size + rows * width),
            transcendentals=0,
        ),
    )(local, cols, a, ext_p)


def per_device(a_blocks, a_cols, a_count, p_blocks, p_cols, q2_blocks, agg3):
    rows_dev = a_cols.shape[0]
    coarse_dev = q2_blocks.shape[0]
    band = coarse_dev * B
    device = lax.axis_index(ALL)
    row_size = lax.axis_size("row")
    group = device // row_size
    f32, bf16 = jnp.float32, jnp.bfloat16

    p_before = passed_along(p_blocks, 1)
    p_after = passed_along(p_blocks, -1)
    near_cols = (p_cols - device * coarse_dev).reshape(-1)
    near_agg = agg3 - group * A3G
    ints = jnp.concatenate([near_agg, near_cols])
    ints = jnp.pad(ints, (0, B * B - ints.shape[0])).astype(bf16)[None, :]
    bundle = jnp.concatenate([q2_blocks, ints], axis=0)
    keep = jnp.arange(KA * B, dtype=jnp.int32)[None, :] < (a_count * B)[:, None]
    amat = jnp.where(keep[:, None, :], a_blocks.reshape(rows_dev, B, KA * B), 0).astype(bf16)
    amat = amat.reshape(rows_dev * B, KA * B)
    bundles = [passed_along(bundle, 1), bundle, passed_along(bundle, -1)]
    late, p_before = lax.optimization_barrier((bundle, p_before))
    bundles = [passed_along(late, 2)] + bundles + [passed_along(late, -2)]
    ext_ints = [part[coarse_dev, : coarse_dev + rows_dev * KP] for part in bundles]
    steps = jnp.arange(5, dtype=jnp.int32)[:, None]
    ext_agg = jnp.stack([x[:coarse_dev] for x in ext_ints]).astype(jnp.int32)
    ext_agg = ext_agg + (device + steps - 2) // row_size * A3G
    ext_agg = ext_agg.reshape(-1)
    ext_cols = jnp.stack([x[coarse_dev:] for x in ext_ints[1:4]]).astype(jnp.int32)
    ext_cols = ext_cols + steps[:3] * coarse_dev
    ext_cols = ext_cols.reshape(-1)
    local = (a_cols - (device - 1) * rows_dev).reshape(-1)
    p_turned = p_blocks.T.reshape(KP, 1, B, rows_dev * B)
    own_t = jnp.repeat((p_cols - device * coarse_dev).T, B, axis=1)
    t_ids = jnp.arange(2 * coarse_dev, dtype=jnp.int32)[:, None, None]
    p_dense = jnp.zeros((2 * coarse_dev, B, rows_dev * B), bf16)
    for m in range(KP):
        p_dense = jnp.where(own_t[m][None, None, :] == t_ids, p_turned[m], p_dense)
    p_dense = p_dense.reshape(2 * band, rows_dev * B)

    ext_q = jnp.concatenate([part[:coarse_dev] for part in bundles], axis=0)
    ext_q = ext_q.reshape(5 * band, B)
    slot = jnp.arange(2 * A3G * B, dtype=jnp.int32) // B
    lanes = (jnp.arange(2 * A3G * B, dtype=jnp.int32) % B)[None, :]
    spread = (jnp.arange(B, dtype=jnp.int32)[:, None] == lanes).astype(bf16)
    wide_q = jnp.dot(ext_q, spread, preferred_element_type=f32).astype(bf16)
    at = ext_agg - group * A3G
    outside = (at < 0) | (at >= A3G)
    at = jnp.where(outside, A3G + jnp.where(at < 0, at + A3G, at - A3G), at)
    at = jnp.repeat(at, B)
    window = jnp.where(at[:, None] == slot[None, :], wide_q, 0).astype(bf16)
    local, amat, p_dense = lax.optimization_barrier((local, amat, p_dense))
    ext_p = jnp.concatenate([p_before, p_blocks, p_after], axis=0)
    w = w_rows(amat, local, ext_cols, ext_p, 4 * band)
    part = jnp.dot(p_dense[band:], w, preferred_element_type=f32).astype(bf16)
    sent = passed_along(part, 1)
    own = jnp.dot(p_dense[:band], w, preferred_element_type=f32)
    own, window = lax.optimization_barrier((own, window))
    level2 = jnp.pad(own, ((0, 0), (band, 0))) + jnp.pad(sent.astype(f32), ((0, 0), (0, band)))
    coarse = level2.astype(bf16)

    v = jnp.dot(coarse, window, preferred_element_type=f32).astype(bf16)
    own_q = window[2 * band : 3 * band, : A3G * B]
    share = lax.dot_general(own_q, v, (((0,), (0,)), ((), ())), preferred_element_type=f32)

    wide = A3G * B
    share = share.astype(bf16).reshape(row_size, wide // row_size, 2 * wide)
    far = lax.all_to_all(share[:, :, wide:], "row", 0, 0).astype(f32)
    far = jnp.concatenate([far[0] + far[1], far[-2] + far[-1]], axis=1).astype(bf16)
    far, mine = lax.optimization_barrier((far, share[:, :, :wide]))
    far = lax.all_gather(far, "row", axis=0, tiled=True)
    mine = lax.all_to_all(mine, "row", 0, 0).astype(f32)
    mine = jnp.sum(mine, axis=0).astype(bf16)
    mine = lax.all_gather(mine, "row", axis=0, tiled=True)
    level3 = jnp.concatenate([far[:, :wide], mine, far[:, wide:]], axis=1).astype(f32)
    return (coarse, level3)


def solution(mesh):
    in_specs = (
        P(ALL, None),
        P(ALL, None),
        P(ALL),
        P(ALL, None),
        P(ALL, None),
        P(ALL, None),
        P(ALL),
    )
    out_specs = (P(ALL, None), P("grp", None))
    return jax.shard_map(
        per_device, mesh=mesh, in_specs=in_specs, out_specs=out_specs, check_vma=False
    )
```
